32 devices in a mesh: groups: 2 (over y), win: 4 (over z), head: 2 (over x), sub: 2 (over core).
Axes of the slice: x: 2, y: 2, z: 4, core: 2. Of those that a mesh axis runs over, the one named last changes fastest.
Arguments:
- queries: float32 [2048, 6144], P(('groups', 'win'), ('head', 'sub')), parts along dimension 0, may hold values from -6.5 to 6.5
- key_rows: float32 [2048, 6144], P(('groups', 'win'), ('head', 'sub')), parts along dimension 0, may hold values from -6.5 to 6.5
- value_rows: float32 [2048, 6144], P(('groups', 'win'), ('head', 'sub')), parts along dimension 0, may hold values from -6 to 6
- merge_target: int32 [2048], P(('groups', 'win')), parts along dimension 0, may hold values from 0 to 831, as said below
Outputs:
- attended: float32 [2048, 6144], P(('groups', 'win'), ('head', 'sub')), parts along dimension 0
The draws below stay inside these ranges and needn't reach their ends.
There are 2 independent parts, one for each index of `groups`. The reference program is written for one: setup_inputs(seed, part) draws one part's arguments, and reference() takes and returns one part's arrays. A program takes and returns all parts, laid end to end along the dimension named above; each array names one. Nothing has to cross between parts.
Inputs may be any that keep to these rules, and one draw needn't show every extreme that they name: merge_target[r] lies in window merge_target[r] // 208; every merged row is joined by one or more rows; of the rows of one window, at most 64 join merged rows of any one window, exactly 64 join those of some window, and at least 52 join those of every window.
All inputs are finite; a program needn't handle non-finite values.
Results may differ from the reference program's by a relative error of at most 0.0003.
Values sent between devices are 32-bit elements; how exact they have to be, the bound alone decides.
A program may use at most 64 MiB of HBM per device.

```python
import jax
import jax.numpy as jnp
from jax import lax

HEADS = 48
HEAD_DIM = 128
ROWS_PER_WINDOW = 256
WINDOW_TOTAL = 4
MERGED_WINDOW_ROWS = 208
DIM = 6144
ROWS = 1024


def draw_merge_target(key, part):
    base_key = jax.random.fold_in(key, 31)
    perm_key, order_key, offset_key, loose_key = jax.random.split(base_key, 4)
    block_rows = MERGED_WINDOW_ROWS // WINDOW_TOTAL
    spill_rows = (ROWS_PER_WINDOW - MERGED_WINDOW_ROWS) // 4
    role_index = jax.vmap(lambda subkey: jax.random.permutation(subkey, ROWS_PER_WINDOW))(jax.random.split(perm_key, WINDOW_TOTAL)).astype(jnp.int32)
    merged_order = jax.vmap(lambda subkey: jax.random.permutation(subkey, MERGED_WINDOW_ROWS))(jax.random.split(order_key, WINDOW_TOTAL)).astype(jnp.int32)
    shifted_window = jax.random.randint(offset_key, (WINDOW_TOTAL, 1), 1, WINDOW_TOTAL).astype(jnp.int32)
    loose_rows = jax.random.randint(loose_key, (WINDOW_TOTAL, ROWS_PER_WINDOW), 0, MERGED_WINDOW_ROWS).astype(jnp.int32)
    current_window = jnp.arange(WINDOW_TOTAL, dtype=jnp.int32)[:, None]
    band_index = role_index // block_rows
    anchor_win = (current_window - band_index) % WINDOW_TOTAL
    anchor_place = jnp.minimum(role_index, MERGED_WINDOW_ROWS - 1)
    surplus_rank = role_index - MERGED_WINDOW_ROWS
    scatter_window = (current_window + shifted_window + 1 + jnp.maximum(surplus_rank - spill_rows, 0) % (WINDOW_TOTAL - 1)) % WINDOW_TOTAL
    surplus_window = jnp.where(surplus_rank < spill_rows, (current_window + shifted_window) % WINDOW_TOTAL, scatter_window)
    is_anchor = role_index < MERGED_WINDOW_ROWS
    target_win = jnp.where(is_anchor, anchor_win, surplus_window)
    anchor_row = merged_order[anchor_win, anchor_place]
    target_row = jnp.where(is_anchor, anchor_row, loose_rows)
    return (target_win * MERGED_WINDOW_ROWS + target_row).reshape(-1).astype(jnp.int32)


def draw_queries(key, part):
    drawn_key = jax.random.fold_in(key, 41)
    result = jnp.clip(1.8 * jax.random.normal(drawn_key, (ROWS, DIM), jnp.float32), -6.5, 6.5)
    return result


def draw_key_rows(key, part):
    drawn_key = jax.random.fold_in(key, 43)
    result = jnp.clip(1.8 * jax.random.normal(drawn_key, (ROWS, DIM), jnp.float32), -6.5, 6.5)
    return result


def steps_of(key, shape, cuts, smallest, largest):
    def one(dim, blocks):
        draws = jax.random.uniform(jax.random.fold_in(jax.random.fold_in(key, 6), dim), (blocks,), jnp.float32, smallest / len(cuts), largest / len(cuts))
        return jnp.repeat(jnp.exp(draws), shape[dim] // blocks).reshape((-1,) + (1,) * (len(shape) - dim - 1))

    loudness = one(*cuts[0])
    for cut in cuts[1:]:
        loudness = loudness * one(*cut)
    return loudness


def bell_draw(stream_key, shape, scale, bound, shards=(), held_as=jnp.bfloat16):
    values = jax.random.normal(stream_key, shape, jnp.float32) * scale
    if len(shards) > 0:
        values = steps_of(stream_key, shape, shards, -0.22, 0.18) * values
    return jnp.clip(values, min=-bound, max=bound).astype(held_as)


def setup_inputs(seed: int = 0, part: int = 0) -> dict:
    splits = jax.random.split(jax.random.key(seed), 5)
    own_keys = jax.random.split(jax.random.fold_in(splits[4], part), 5)
    return {
        "queries": draw_queries(jax.random.fold_in(jax.random.fold_in(splits[4], part), 71), part),
        "key_rows": draw_key_rows(jax.random.fold_in(jax.random.fold_in(splits[4], part), 71), part),
        "value_rows": bell_draw(own_keys[2], (ROWS, DIM), 1.0, 6.0, ((0, 4), (1, 4)), jnp.float32),
        "merge_target": draw_merge_target(jax.random.fold_in(jax.random.fold_in(splits[4], part), 71), part),
    }


def reference(queries, key_rows, value_rows, merge_target):
    merged_total = WINDOW_TOTAL * MERGED_WINDOW_ROWS
    counts = jax.ops.segment_sum(jnp.ones((ROWS,), jnp.float32), merge_target, merged_total)

    def merge_rows(source):
        return jax.ops.segment_sum(source, merge_target, merged_total) / counts[:, None]

    merged_queries = merge_rows(queries)
    merged_keys = merge_rows(key_rows)
    merged_values = merge_rows(value_rows)
    scaling = 1.0 / (HEAD_DIM ** 0.5)

    def one_head(head_index):
        column = (head_index * HEAD_DIM).astype(jnp.int32)
        query_head = lax.dynamic_slice_in_dim(merged_queries, column, HEAD_DIM, 1)
        key_head = lax.dynamic_slice_in_dim(merged_keys, column, HEAD_DIM, 1)
        value_head = lax.dynamic_slice_in_dim(merged_values, column, HEAD_DIM, 1)

        def one_window(window_index):
            first = (window_index * MERGED_WINDOW_ROWS).astype(jnp.int32)
            query_block = lax.dynamic_slice_in_dim(query_head, first, MERGED_WINDOW_ROWS, 0)
            scores = jnp.dot(query_block, key_head.T, precision=lax.Precision.HIGHEST) * scaling
            top_score = jnp.max(scores, axis=1, keepdims=True)
            attention_weight = jnp.exp(scores - top_score)
            mixed = jnp.dot(attention_weight, value_head, precision=lax.Precision.HIGHEST)
            return mixed / jnp.sum(attention_weight, axis=1, keepdims=True)

        return lax.map(one_window, jnp.arange(WINDOW_TOTAL, dtype=jnp.int32)).reshape(merged_total, HEAD_DIM)

    per_head = lax.map(one_head, jnp.arange(HEADS, dtype=jnp.int32))
    merged_output = jnp.transpose(per_head, (1, 0, 2)).reshape(merged_total, DIM)
    return merged_output[merge_target]
```

```python
import functools
import math

import jax
import jax.numpy as jnp
from jax import lax
from jax.experimental import pallas as pl
from jax.experimental.pallas import tpu as pltpu
from jax.sharding import PartitionSpec as P

HEAD_DIM = 128
MERGED_WINDOW_ROWS = 208
SCALING = 1.0 / math.sqrt(HEAD_DIM)
F32 = jnp.float32
BF16 = jnp.bfloat16
MESH = pl.DeviceIdType.MESH


def halves(x):
    high = x.astype(BF16)
    return high, (x - high.astype(F32)).astype(BF16)


def dot(a, b, dims=((1,), (0,))):
    return lax.dot_general(a, b, (dims, ((), ())), preferred_element_type=F32)


def partners_of(me, window_count):
    if window_count == 4:
        return [lax.rem(me + 2, 4), 3 - me, me + 1 - 2 * lax.rem(me, 2)]
    return [lax.rem(me + o, window_count) for o in range(1, window_count)]


def kernel(
    window_count, slots, rows,
    q_ref, k_ref, v_ref, mt_ref, out_ref,
    inbox, outbox, targets, member, same, key_parts, value_parts,
    own_sem, in_send, in_recv, mt_send, mt_recv, out_own, out_send, out_recv,
):
    me = lax.axis_index("win")
    partners = partners_of(me, window_count)
    sources = (q_ref, k_ref, v_ref)
    merged_total = window_count * MERGED_WINDOW_ROWS

    def head_columns(window, slot):
        return pl.ds(pl.multiple_of((window * slots + slot) * HEAD_DIM, HEAD_DIM), HEAD_DIM)

    def own_copy(slot, t):
        return pltpu.make_async_copy(
            sources[t].at[:, head_columns(me, slot)],
            inbox.at[slot, t, pl.ds(pl.multiple_of(me * rows, rows), rows)],
            own_sem.at[slot, t],
        )

    def send_copy(slot, t, to):
        return pltpu.make_async_remote_copy(
            src_ref=sources[t].at[:, head_columns(to, slot)],
            dst_ref=inbox.at[slot, t, pl.ds(pl.multiple_of(me * rows, rows), rows)],
            send_sem=in_send.at[slot, t, to],
            recv_sem=in_recv.at[slot, t, me],
            device_id={"win": to},
            device_id_type=MESH,
        )

    def arrival(slot, t, source):
        return pltpu.make_async_remote_copy(
            src_ref=sources[t].at[:, head_columns(me, slot)],
            dst_ref=inbox.at[slot, t, pl.ds(pl.multiple_of(source * rows, rows), rows)],
            send_sem=in_send.at[slot, t, source],
            recv_sem=in_recv.at[slot, t, source],
            device_id={"win": source},
            device_id_type=MESH,
        )

    def mt_copy(to, slot_of):
        return pltpu.make_async_remote_copy(
            src_ref=mt_ref,
            dst_ref=targets.at[slot_of],
            send_sem=mt_send.at[to],
            recv_sem=mt_recv.at[slot_of],
            device_id={"win": to},
            device_id_type=MESH,
        )

    def return_copy(slot, to):
        return pltpu.make_async_remote_copy(
            src_ref=outbox.at[slot, pl.ds(pl.multiple_of(to * rows, rows), rows)],
            dst_ref=out_ref.at[:, head_columns(me, slot)],
            send_sem=out_send.at[slot, to],
            recv_sem=out_recv.at[slot, me],
            device_id={"win": to},
            device_id_type=MESH,
        )

    def return_arrival(slot, source):
        return pltpu.make_async_remote_copy(
            src_ref=outbox.at[slot, pl.ds(pl.multiple_of(source * rows, rows), rows)],
            dst_ref=out_ref.at[:, head_columns(source, slot)],
            send_sem=out_send.at[slot, source],
            recv_sem=out_recv.at[slot, source],
            device_id={"win": source},
            device_id_type=MESH,
        )

    def return_own(slot):
        return pltpu.make_async_copy(
            outbox.at[slot, pl.ds(pl.multiple_of(me * rows, rows), rows)],
            out_ref.at[:, head_columns(me, slot)],
            out_own.at[slot],
        )

    barrier = pltpu.get_barrier_semaphore()
    for other in partners:
        pl.semaphore_signal(barrier, inc=1, device_id={"win": other}, device_id_type=MESH)
    for slot in range(slots):
        for t in range(3):
            own_copy(slot, t).start()
    pl.semaphore_wait(barrier, window_count - 1)

    for other in partners:
        mt_copy(other, me).start()
    for slot in range(slots):
        for t in (1, 0, 2):
            for other in partners:
                send_copy(slot, t, other).start()

    targets[me] = mt_ref[...]
    for other in partners:
        mt_copy(other, other).wait_recv()
    merged_index = lax.broadcasted_iota(jnp.int32, (merged_total, rows), 0)
    for w in range(window_count):
        member[:, w * rows : (w + 1) * rows] = (
            (merged_index == targets[w]).astype(F32).astype(BF16)
        )
    for w in range(window_count):
        column = jnp.transpose(
            jnp.broadcast_to(targets[w].astype(F32), (HEAD_DIM, rows))
        )[:, :1]
        for u in range(window_count):
            same[w * rows : (w + 1) * rows, u * rows : (u + 1) * rows] = (
                (column == targets[u].astype(F32)).astype(F32).astype(BF16)
            )

    def merge(matrix, source):
        high, low = halves(source)
        total = dot(matrix, high) + dot(matrix, low)
        count = jnp.sum(matrix.astype(F32), axis=1, keepdims=True)
        return total / count

    def one_slot(slot, carry):
        for t in range(3):
            own_copy(slot, t).wait()
            for other in partners:
                arrival(slot, t, other).wait_recv()
        for t, parts in ((1, key_parts), (2, value_parts)):
            high, low = halves(merge(member[...], inbox[slot, t]))
            parts[0] = high
            parts[1] = low

        def one_window(i, carry):
            w = lax.rem(me + 1 + i, window_count)
            chosen = pl.ds(pl.multiple_of(w * rows, rows), rows)
            query = merge(same[chosen], inbox[slot, 0]) * SCALING
            q_high, q_low = halves(query)
            over = ((1,), (1,))
            scores = (
                dot(q_high, key_parts[0], over)
                + dot(q_high, key_parts[1], over)
                + dot(q_low, key_parts[0], over)
            )
            top = jnp.max(scores, axis=1, keepdims=True)
            weight = jnp.exp(scores - top)
            total = jnp.sum(weight, axis=1, keepdims=True)
            w_high, w_low = halves(weight)
            mixed = (
                dot(w_high, value_parts[0])
                + dot(w_high, value_parts[1])
                + dot(w_low, value_parts[0])
            )
            outbox[slot, chosen] = mixed / total

            @pl.when(i < window_count - 1)
            def _():
                return_copy(slot, w).start()

            return carry

        lax.fori_loop(0, window_count, one_window, 0)
        return_own(slot).start()
        return carry

    lax.fori_loop(0, slots, one_slot, 0)

    for other in partners:
        mt_copy(other, me).wait_send()
    for slot in range(slots):
        for t in range(3):
            for other in partners:
                send_copy(slot, t, other).wait_send()
        return_own(slot).wait()
        for other in partners:
            return_copy(slot, other).wait_send()
            return_arrival(slot, other).wait_recv()


def by_heads(queries, key_rows, value_rows, merge_target):
    window_count = lax.axis_size("win")
    rows, col_width = queries.shape
    slots = col_width // HEAD_DIM // window_count
    all_rows = window_count * rows
    merged_total = window_count * MERGED_WINDOW_ROWS
    dma = pltpu.SemaphoreType.DMA
    hbm = pl.BlockSpec(memory_space=pl.ANY)
    flops = 2 * slots * HEAD_DIM * all_rows * (6 * merged_total + 4 * merged_total + 2 * all_rows)
    return pl.pallas_call(
        functools.partial(kernel, window_count, slots, rows),
        out_shape=jax.ShapeDtypeStruct((rows, col_width), F32),
        in_specs=[hbm, hbm, hbm, pl.BlockSpec(memory_space=pltpu.VMEM)],
        out_specs=hbm,
        scratch_shapes=[
            pltpu.VMEM((slots, 3, all_rows, HEAD_DIM), F32),
            pltpu.VMEM((slots, all_rows, HEAD_DIM), F32),
            pltpu.VMEM((window_count, 1, rows), jnp.int32),
            pltpu.VMEM((merged_total, all_rows), BF16),
            pltpu.VMEM((all_rows, all_rows), BF16),
            pltpu.VMEM((2, merged_total, HEAD_DIM), BF16),
            pltpu.VMEM((2, merged_total, HEAD_DIM), BF16),
            dma((slots, 3)),
            dma((slots, 3, window_count)),
            dma((slots, 3, window_count)),
            dma((window_count,)),
            dma((window_count,)),
            dma((slots,)),
            dma((slots, window_count)),
            dma((slots, window_count)),
        ],
        compiler_params=pltpu.CompilerParams(
            collective_id=0, has_side_effects=True, vmem_limit_bytes=48 * 1024 * 1024
        ),
        cost_estimate=pl.CostEstimate(
            flops=flops, bytes_accessed=32 * rows * col_width, transcendentals=0
        ),
    )(queries, key_rows, value_rows, merge_target.reshape(1, rows))


def exact_dot(a, b):
    return jnp.dot(a, b, precision=lax.Precision.HIGHEST)


def by_rows(queries, key_rows, value_rows, merge_target):
    window_count = lax.axis_size("win")
    head_count = queries.shape[1] // HEAD_DIM
    rows = queries.shape[0]
    gathered = [
        lax.all_gather(x, "win", axis=0, tiled=True)
        for x in (queries, key_rows, value_rows, merge_target)
    ]
    all_queries, all_keys, all_values, all_targets = gathered

    def merged_window(window):
        index = window * MERGED_WINDOW_ROWS + jnp.arange(MERGED_WINDOW_ROWS, dtype=jnp.int32)
        member = (index[:, None] == all_targets[None, :]).astype(F32)
        count = jnp.sum(member, axis=1, keepdims=True)
        return exact_dot(member, all_keys) / count, exact_dot(member, all_values) / count

    merged_keys, merged_values = lax.map(merged_window, jnp.arange(window_count, dtype=jnp.int32))
    same = (merge_target[:, None] == all_targets[None, :]).astype(F32)
    own_queries = exact_dot(same, all_queries) / jnp.sum(same, axis=1, keepdims=True)

    def by_head(x):
        return jnp.transpose(x.reshape(-1, head_count, HEAD_DIM), (1, 0, 2))

    def one_head(stack):
        query, key, value = stack
        scores = exact_dot(query, key.T) * SCALING
        weight = jnp.exp(scores - jnp.max(scores, axis=1, keepdims=True))
        return exact_dot(weight, value) / jnp.sum(weight, axis=1, keepdims=True)

    mixed = lax.map(one_head, (by_head(own_queries), by_head(merged_keys), by_head(merged_values)))
    return jnp.transpose(mixed, (1, 0, 2)).reshape(rows, -1)


def local(queries, key_rows, value_rows, merge_target):
    heads = queries.shape[1] // HEAD_DIM
    if heads % lax.axis_size("win") == 0:
        return by_heads(queries, key_rows, value_rows, merge_target)
    return by_rows(queries, key_rows, value_rows, merge_target)


def solution(mesh):
    rows = P(("groups", "win"), ("head", "sub"))
    return jax.shard_map(
        local,
        mesh=mesh,
        in_specs=(rows, rows, rows, P(("groups", "win"))),
        out_specs=rows,
        check_vma=False,
    )
```

```python
import functools
import math

import jax
import jax.numpy as jnp
from jax import lax
from jax.experimental import pallas as pl
from jax.experimental.pallas import tpu as pltpu
from jax.sharding import PartitionSpec as P

HEAD_DIM = 128
MERGED_WINDOW_ROWS = 208
SCALING = 1.0 / math.sqrt(HEAD_DIM)
F32 = jnp.float32
BF16 = jnp.bfloat16
MESH = pl.DeviceIdType.MESH


def halves(x):
    high = x.astype(BF16)
    return high, (x - high.astype(F32)).astype(BF16)


def dot(a, b, dims=((1,), (0,))):
    return lax.dot_general(a, b, (dims, ((), ())), preferred_element_type=F32)


def partners_of(me, window_count):
    if window_count == 4:
        return [lax.rem(me + 2, 4), 3 - me, me + 1 - 2 * lax.rem(me, 2)]
    return [lax.rem(me + o, window_count) for o in range(1, window_count)]


def kernel(
    window_count, slots, rows,
    q_ref, k_ref, v_ref, mt_ref, out_ref,
    inbox, outbox, targets, member, same, key_parts, value_parts,
    mt_own, own_sem, in_send, in_recv, mt_send, mt_recv, out_own, out_send, out_recv,
):
    me = lax.axis_index("win")
    partners = partners_of(me, window_count)
    sources = (q_ref, k_ref, v_ref)
    merged_total = window_count * MERGED_WINDOW_ROWS

    def head_columns(window, slot):
        return pl.ds(pl.multiple_of((window * slots + slot) * HEAD_DIM, HEAD_DIM), HEAD_DIM)

    def own_copy(slot, t):
        return pltpu.make_async_copy(
            sources[t].at[:, head_columns(me, slot)],
            inbox.at[slot, t, pl.ds(pl.multiple_of(me * rows, rows), rows)],
            own_sem.at[slot, t],
        )

    def send_copy(slot, t, to):
        return pltpu.make_async_remote_copy(
            src_ref=sources[t].at[:, head_columns(to, slot)],
            dst_ref=inbox.at[slot, t, pl.ds(pl.multiple_of(me * rows, rows), rows)],
            send_sem=in_send.at[slot, t, to],
            recv_sem=in_recv.at[slot, t, me],
            device_id={"win": to},
            device_id_type=MESH,
        )

    def arrival(slot, t, source):
        return pltpu.make_async_remote_copy(
            src_ref=sources[t].at[:, head_columns(me, slot)],
            dst_ref=inbox.at[slot, t, pl.ds(pl.multiple_of(source * rows, rows), rows)],
            send_sem=in_send.at[slot, t, source],
            recv_sem=in_recv.at[slot, t, source],
            device_id={"win": source},
            device_id_type=MESH,
        )

    def mt_copy(to, slot_of):
        return pltpu.make_async_remote_copy(
            src_ref=mt_ref,
            dst_ref=targets.at[slot_of],
            send_sem=mt_send.at[to],
            recv_sem=mt_recv.at[slot_of],
            device_id={"win": to},
            device_id_type=MESH,
        )

    def return_copy(slot, to):
        return pltpu.make_async_remote_copy(
            src_ref=outbox.at[slot, pl.ds(pl.multiple_of(to * rows, rows), rows)],
            dst_ref=out_ref.at[:, head_columns(me, slot)],
            send_sem=out_send.at[slot, to],
            recv_sem=out_recv.at[slot, me],
            device_id={"win": to},
            device_id_type=MESH,
        )

    def return_arrival(slot, source):
        return pltpu.make_async_remote_copy(
            src_ref=outbox.at[slot, pl.ds(pl.multiple_of(source * rows, rows), rows)],
            dst_ref=out_ref.at[:, head_columns(source, slot)],
            send_sem=out_send.at[slot, source],
            recv_sem=out_recv.at[slot, source],
            device_id={"win": source},
            device_id_type=MESH,
        )

    def return_own(slot):
        return pltpu.make_async_copy(
            outbox.at[slot, pl.ds(pl.multiple_of(me * rows, rows), rows)],
            out_ref.at[:, head_columns(me, slot)],
            out_own.at[slot],
        )

    mt_mine = pltpu.make_async_copy(mt_ref, targets.at[me], mt_own)
    barrier = pltpu.get_barrier_semaphore()
    for other in partners:
        pl.semaphore_signal(barrier, inc=1, device_id={"win": other}, device_id_type=MESH)
    mt_mine.start()
    for slot in range(slots):
        for t in range(3):
            own_copy(slot, t).start()
    pl.semaphore_wait(barrier, window_count - 1)

    for other in partners:
        mt_copy(other, me).start()
    for slot in range(slots):
        for t in (1, 0, 2):
            for other in partners:
                send_copy(slot, t, other).start()

    mt_mine.wait()
    for other in partners:
        mt_copy(other, other).wait_recv()
    merged_index = lax.broadcasted_iota(jnp.int32, (merged_total, rows), 0)
    for w in range(window_count):
        member[:, w * rows : (w + 1) * rows] = (
            (merged_index == targets[w]).astype(F32).astype(BF16)
        )
    for w in range(window_count):
        column = jnp.transpose(
            jnp.broadcast_to(targets[w].astype(F32), (HEAD_DIM, rows))
        )[:, :1]
        for u in range(window_count):
            same[w * rows : (w + 1) * rows, u * rows : (u + 1) * rows] = (
                (column == targets[u].astype(F32)).astype(F32).astype(BF16)
            )

    def merge(matrix, source):
        high, low = halves(source)
        total = dot(matrix, high) + dot(matrix, low)
        count = jnp.sum(matrix.astype(F32), axis=1, keepdims=True)
        return total / count

    def one_slot(slot, carry):
        for t in range(3):
            own_copy(slot, t).wait()
            for other in partners:
                arrival(slot, t, other).wait_recv()
        for t, parts in ((1, key_parts), (2, value_parts)):
            high, low = halves(merge(member[...], inbox[slot, t]))
            parts[0] = high
            parts[1] = low

        def one_window(i, carry):
            w = lax.rem(me + 1 + i, window_count)
            chosen = pl.ds(pl.multiple_of(w * rows, rows), rows)
            query = merge(same[chosen], inbox[slot, 0]) * SCALING
            q_high, q_low = halves(query)
            over = ((1,), (1,))
            scores = (
                dot(q_high, key_parts[0], over)
                + dot(q_high, key_parts[1], over)
                + dot(q_low, key_parts[0], over)
            )
            top = jnp.max(scores, axis=1, keepdims=True)
            weight = jnp.exp(scores - top)
            total = jnp.sum(weight, axis=1, keepdims=True)
            w_high, w_low = halves(weight)
            mixed = (
                dot(w_high, value_parts[0])
                + dot(w_high, value_parts[1])
                + dot(w_low, value_parts[0])
            )
            outbox[slot, chosen] = mixed / total

            @pl.when(i < window_count - 1)
            def _():
                return_copy(slot, w).start()

            return carry

        lax.fori_loop(0, window_count, one_window, 0)
        return_own(slot).start()
        return carry

    lax.fori_loop(0, slots, one_slot, 0)

    for other in partners:
        mt_copy(other, me).wait_send()
    for slot in range(slots):
        for t in range(3):
            for other in partners:
                send_copy(slot, t, other).wait_send()
        return_own(slot).wait()
        for other in partners:
            return_copy(slot, other).wait_send()
            return_arrival(slot, other).wait_recv()


def by_heads(queries, key_rows, value_rows, merge_target):
    window_count = lax.axis_size("win")
    rows, col_width = queries.shape
    slots = col_width // HEAD_DIM // window_count
    all_rows = window_count * rows
    merged_total = window_count * MERGED_WINDOW_ROWS
    dma = pltpu.SemaphoreType.DMA
    hbm = pl.BlockSpec(memory_space=pl.ANY)
    flops = 2 * slots * HEAD_DIM * all_rows * (6 * merged_total + 4 * merged_total + 2 * all_rows)
    return pl.pallas_call(
        functools.partial(kernel, window_count, slots, rows),
        out_shape=jax.ShapeDtypeStruct((rows, col_width), F32),
        in_specs=[hbm] * 4,
        out_specs=hbm,
        scratch_shapes=[
            pltpu.VMEM((slots, 3, all_rows, HEAD_DIM), F32),
            pltpu.VMEM((slots, all_rows, HEAD_DIM), F32),
            pltpu.VMEM((window_count, 1, rows), jnp.int32),
            pltpu.VMEM((merged_total, all_rows), BF16),
            pltpu.VMEM((all_rows, all_rows), BF16),
            pltpu.VMEM((2, merged_total, HEAD_DIM), BF16),
            pltpu.VMEM((2, merged_total, HEAD_DIM), BF16),
            dma,
            dma((slots, 3)),
            dma((slots, 3, window_count)),
            dma((slots, 3, window_count)),
            dma((window_count,)),
            dma((window_count,)),
            dma((slots,)),
            dma((slots, window_count)),
            dma((slots, window_count)),
        ],
        compiler_params=pltpu.CompilerParams(
            collective_id=0, has_side_effects=True, vmem_limit_bytes=63 * 1024 * 1024
        ),
        cost_estimate=pl.CostEstimate(
            flops=flops, bytes_accessed=32 * rows * col_width, transcendentals=0
        ),
    )(queries, key_rows, value_rows, merge_target.reshape(1, rows))


def exact_dot(a, b):
    return jnp.dot(a, b, precision=lax.Precision.HIGHEST)


def by_rows(queries, key_rows, value_rows, merge_target):
    window_count = lax.axis_size("win")
    head_count = queries.shape[1] // HEAD_DIM
    rows = queries.shape[0]
    gathered = [
        lax.all_gather(x, "win", axis=0, tiled=True)
        for x in (queries, key_rows, value_rows, merge_target)
    ]
    all_queries, all_keys, all_values, all_targets = gathered

    def merged_window(window):
        index = window * MERGED_WINDOW_ROWS + jnp.arange(MERGED_WINDOW_ROWS, dtype=jnp.int32)
        member = (index[:, None] == all_targets[None, :]).astype(F32)
        count = jnp.sum(member, axis=1, keepdims=True)
        return exact_dot(member, all_keys) / count, exact_dot(member, all_values) / count

    merged_keys, merged_values = lax.map(merged_window, jnp.arange(window_count, dtype=jnp.int32))
    same = (merge_target[:, None] == all_targets[None, :]).astype(F32)
    own_queries = exact_dot(same, all_queries) / jnp.sum(same, axis=1, keepdims=True)

    def by_head(x):
        return jnp.transpose(x.reshape(-1, head_count, HEAD_DIM), (1, 0, 2))

    def one_head(stack):
        query, key, value = stack
        scores = exact_dot(query, key.T) * SCALING
        weight = jnp.exp(scores - jnp.max(scores, axis=1, keepdims=True))
        return exact_dot(weight, value) / jnp.sum(weight, axis=1, keepdims=True)

    mixed = lax.map(one_head, (by_head(own_queries), by_head(merged_keys), by_head(merged_values)))
    return jnp.transpose(mixed, (1, 0, 2)).reshape(rows, -1)


def local(queries, key_rows, value_rows, merge_target):
    heads = queries.shape[1] // HEAD_DIM
    if heads % lax.axis_size("win") == 0:
        return by_heads(queries, key_rows, value_rows, merge_target)
    return by_rows(queries, key_rows, value_rows, merge_target)


def solution(mesh):
    rows = P(("groups", "win"), ("head", "sub"))
    return jax.shard_map(
        local,
        mesh=mesh,
        in_specs=(rows, rows, rows, P(("groups", "win"))),
        out_specs=rows,
        check_vma=False,
    )
```

```python
import functools
import math

import jax
import jax.numpy as jnp
from jax import lax
from jax.experimental import pallas as pl
from jax.experimental.pallas import tpu as pltpu
from jax.sharding import PartitionSpec as P

HEAD_DIM = 128
MERGED_WINDOW_ROWS = 208
SCALING = 1.0 / math.sqrt(HEAD_DIM)
F32 = jnp.float32
BF16 = jnp.bfloat16
MESH = pl.DeviceIdType.MESH


def halves(x):
    high = x.astype(BF16)
    return high, (x - high.astype(F32)).astype(BF16)


def dot(a, b, dims=((1,), (0,))):
    return lax.dot_general(a, b, (dims, ((), ())), preferred_element_type=F32)


def partners_of(me, window_count):
    if window_count == 4:
        return [lax.rem(me + 2, 4), 3 - me, me + 1 - 2 * lax.rem(me, 2)]
    return [lax.rem(me + o, window_count) for o in range(1, window_count)]


def kernel(
    window_count, slots, rows,
    q_ref, k_ref, v_ref, mt_ref, out_ref,
    inbox, outbox, targets, member, same, key_parts, value_parts,
    mt_own, own_sem, in_send, in_recv, mt_send, mt_recv, out_own, out_send, out_recv,
):
    me = lax.axis_index("win")
    partners = partners_of(me, window_count)
    sources = (q_ref, k_ref, v_ref)
    merged_total = window_count * MERGED_WINDOW_ROWS

    def head_columns(window, slot):
        return pl.ds(pl.multiple_of((window * slots + slot) * HEAD_DIM, HEAD_DIM), HEAD_DIM)

    def own_copy(slot, t):
        return pltpu.make_async_copy(
            sources[t].at[:, head_columns(me, slot)],
            inbox.at[slot, t, pl.ds(pl.multiple_of(me * rows, rows), rows)],
            own_sem.at[slot, t],
        )

    def send_copy(slot, t, to):
        return pltpu.make_async_remote_copy(
            src_ref=sources[t].at[:, head_columns(to, slot)],
            dst_ref=inbox.at[slot, t, pl.ds(pl.multiple_of(me * rows, rows), rows)],
            send_sem=in_send.at[slot, t, to],
            recv_sem=in_recv.at[slot, t, me],
            device_id={"win": to},
            device_id_type=MESH,
        )

    def arrival(slot, t, source):
        return pltpu.make_async_remote_copy(
            src_ref=sources[t].at[:, head_columns(me, slot)],
            dst_ref=inbox.at[slot, t, pl.ds(pl.multiple_of(source * rows, rows), rows)],
            send_sem=in_send.at[slot, t, source],
            recv_sem=in_recv.at[slot, t, source],
            device_id={"win": source},
            device_id_type=MESH,
        )

    def mt_copy(to, slot_of):
        return pltpu.make_async_remote_copy(
            src_ref=mt_ref,
            dst_ref=targets.at[slot_of],
            send_sem=mt_send.at[to],
            recv_sem=mt_recv.at[slot_of],
            device_id={"win": to},
            device_id_type=MESH,
        )

    def return_copy(slot, to):
        return pltpu.make_async_remote_copy(
            src_ref=outbox.at[slot, pl.ds(pl.multiple_of(to * rows, rows), rows)],
            dst_ref=out_ref.at[:, head_columns(me, slot)],
            send_sem=out_send.at[slot, to],
            recv_sem=out_recv.at[slot, me],
            device_id={"win": to},
            device_id_type=MESH,
        )

    def return_arrival(slot, source):
        return pltpu.make_async_remote_copy(
            src_ref=outbox.at[slot, pl.ds(pl.multiple_of(source * rows, rows), rows)],
            dst_ref=out_ref.at[:, head_columns(source, slot)],
            send_sem=out_send.at[slot, source],
            recv_sem=out_recv.at[slot, source],
            device_id={"win": source},
            device_id_type=MESH,
        )

    def return_own(slot):
        return pltpu.make_async_copy(
            outbox.at[slot, pl.ds(pl.multiple_of(me * rows, rows), rows)],
            out_ref.at[:, head_columns(me, slot)],
            out_own.at[slot],
        )

    mt_mine = pltpu.make_async_copy(mt_ref, targets.at[me], mt_own)
    barrier = pltpu.get_barrier_semaphore()
    for other in partners:
        pl.semaphore_signal(barrier, inc=1, device_id={"win": other}, device_id_type=MESH)
    mt_mine.start()
    for slot in range(slots):
        for t in range(3):
            own_copy(slot, t).start()
    pl.semaphore_wait(barrier, window_count - 1)

    for other in partners:
        mt_copy(other, me).start()
    for slot in range(slots):
        for t in (1, 0, 2):
            for other in partners:
                send_copy(slot, t, other).start()

    mt_mine.wait()
    for other in partners:
        mt_copy(other, other).wait_recv()
    merged_index = lax.broadcasted_iota(jnp.int32, (merged_total, rows), 0)
    for w in range(window_count):
        member[:, w * rows : (w + 1) * rows] = (
            (merged_index == targets[w]).astype(F32).astype(BF16)
        )
    for w in range(window_count):
        column = jnp.transpose(
            jnp.broadcast_to(targets[w].astype(F32), (HEAD_DIM, rows))
        )[:, :1]
        for u in range(window_count):
            same[w * rows : (w + 1) * rows, u * rows : (u + 1) * rows] = (
                (column == targets[u].astype(F32)).astype(F32).astype(BF16)
            )

    def merge(matrix, source):
        high, low = halves(source)
        total = dot(matrix, high) + dot(matrix, low)
        count = jnp.sum(matrix.astype(F32), axis=1, keepdims=True)
        return total / count

    def one_slot(slot, carry):
        for t in range(3):
            own_copy(slot, t).wait()
            for other in partners:
                arrival(slot, t, other).wait_recv()
        for t, parts in ((1, key_parts), (2, value_parts)):
            high, low = halves(merge(member[...], inbox[slot, t]))
            parts[0] = high
            parts[1] = low

        def one_window(i, carry):
            w = lax.rem(me + 1 + i, window_count)
            chosen = pl.ds(pl.multiple_of(w * rows, rows), rows)
            query = merge(same[chosen], inbox[slot, 0]) * SCALING
            q_high, q_low = halves(query)
            over = ((1,), (1,))
            scores = (
                dot(q_high, key_parts[0], over)
                + dot(q_high, key_parts[1], over)
                + dot(q_low, key_parts[0], over)
            )
            top = jnp.max(scores, axis=1, keepdims=True)
            weight = jnp.exp(scores - top)
            total = jnp.sum(weight, axis=1, keepdims=True)
            w_high, w_low = halves(weight)
            mixed = (
                dot(w_high, value_parts[0])
                + dot(w_high, value_parts[1])
                + dot(w_low, value_parts[0])
            )
            outbox[slot, chosen] = mixed / total

            @pl.when(i < window_count - 1)
            def _():
                return_copy(slot, w).start()

            return carry

        lax.fori_loop(0, window_count, one_window, 0)
        return_own(slot).start()
        return carry

    lax.fori_loop(0, slots, one_slot, 0)

    for other in partners:
        mt_copy(other, me).wait_send()
    for slot in range(slots):
        for t in range(3):
            for other in partners:
                send_copy(slot, t, other).wait_send()
        return_own(slot).wait()
        for other in partners:
            return_copy(slot, other).wait_send()
            return_arrival(slot, other).wait_recv()


def by_heads(queries, key_rows, value_rows, merge_target):
    window_count = lax.axis_size("win")
    rows, col_width = queries.shape
    slots = col_width // HEAD_DIM // window_count
    all_rows = window_count * rows
    merged_total = window_count * MERGED_WINDOW_ROWS
    dma = pltpu.SemaphoreType.DMA
    hbm = pl.BlockSpec(memory_space=pl.ANY)
    flops = 2 * slots * HEAD_DIM * all_rows * (6 * merged_total + 4 * merged_total + 2 * all_rows)
    return pl.pallas_call(
        functools.partial(kernel, window_count, slots, rows),
        out_shape=pltpu.VMEM((rows, col_width), F32),
        in_specs=[hbm] * 4,
        out_specs=hbm,
        scratch_shapes=[
            pltpu.VMEM((slots, 3, all_rows, HEAD_DIM), F32),
            pltpu.VMEM((slots, all_rows, HEAD_DIM), F32),
            pltpu.VMEM((window_count, 1, rows), jnp.int32),
            pltpu.VMEM((merged_total, all_rows), BF16),
            pltpu.VMEM((all_rows, all_rows), BF16),
            pltpu.VMEM((2, merged_total, HEAD_DIM), BF16),
            pltpu.VMEM((2, merged_total, HEAD_DIM), BF16),
            dma,
            dma((slots, 3)),
            dma((slots, 3, window_count)),
            dma((slots, 3, window_count)),
            dma((window_count,)),
            dma((window_count,)),
            dma((slots,)),
            dma((slots, window_count)),
            dma((slots, window_count)),
        ],
        compiler_params=pltpu.CompilerParams(
            collective_id=0, has_side_effects=True, vmem_limit_bytes=60 * 1024 * 1024
        ),
        cost_estimate=pl.CostEstimate(
            flops=flops, bytes_accessed=32 * rows * col_width, transcendentals=0
        ),
    )(queries, key_rows, value_rows, merge_target.reshape(1, rows))


def exact_dot(a, b):
    return jnp.dot(a, b, precision=lax.Precision.HIGHEST)


def by_rows(queries, key_rows, value_rows, merge_target):
    window_count = lax.axis_size("win")
    head_count = queries.shape[1] // HEAD_DIM
    rows = queries.shape[0]
    gathered = [
        lax.all_gather(x, "win", axis=0, tiled=True)
        for x in (queries, key_rows, value_rows, merge_target)
    ]
    all_queries, all_keys, all_values, all_targets = gathered

    def merged_window(window):
        index = window * MERGED_WINDOW_ROWS + jnp.arange(MERGED_WINDOW_ROWS, dtype=jnp.int32)
        member = (index[:, None] == all_targets[None, :]).astype(F32)
        count = jnp.sum(member, axis=1, keepdims=True)
        return exact_dot(member, all_keys) / count, exact_dot(member, all_values) / count

    merged_keys, merged_values = lax.map(merged_window, jnp.arange(window_count, dtype=jnp.int32))
    same = (merge_target[:, None] == all_targets[None, :]).astype(F32)
    own_queries = exact_dot(same, all_queries) / jnp.sum(same, axis=1, keepdims=True)

    def by_head(x):
        return jnp.transpose(x.reshape(-1, head_count, HEAD_DIM), (1, 0, 2))

    def one_head(stack):
        query, key, value = stack
        scores = exact_dot(query, key.T) * SCALING
        weight = jnp.exp(scores - jnp.max(scores, axis=1, keepdims=True))
        return exact_dot(weight, value) / jnp.sum(weight, axis=1, keepdims=True)

    mixed = lax.map(one_head, (by_head(own_queries), by_head(merged_keys), by_head(merged_values)))
    return jnp.transpose(mixed, (1, 0, 2)).reshape(rows, -1)


def local(queries, key_rows, value_rows, merge_target):
    heads = queries.shape[1] // HEAD_DIM
    if heads % lax.axis_size("win") == 0:
        return by_heads(queries, key_rows, value_rows, merge_target)
    return by_rows(queries, key_rows, value_rows, merge_target)


def solution(mesh):
    rows = P(("groups", "win"), ("head", "sub"))
    return jax.shard_map(
        local,
        mesh=mesh,
        in_specs=(rows, rows, rows, P(("groups", "win"))),
        out_specs=rows,
        check_vma=False,
    )
```
